512 devices in a mesh: rep: 16 (over y, z_hi), fsdp: 8 (over x, core), tp: 4 (over z_lo).
Axes of the slice: x: 4, y: 8, z: 8 (z_hi: 2, z_lo: 4; z = z_hi * 4 + z_lo), core: 2. Of those that a mesh axis runs over, the one named last changes fastest.
Arguments:
- tokens: bfloat16 [16, 2048, 4096], P('rep', 'fsdp', 'tp'), may hold values from -6 to 6
- key_weight: float32 [16, 4096, 1024], P('rep', 'fsdp', 'tp'), may hold values from -6 to 6
- value_weight: float32 [16, 4096, 1024], P('rep', 'fsdp', 'tp'), may hold values from -6 to 6
- key_momentum: float32 [16, 4096, 1024], P('rep', 'fsdp', 'tp'), may hold values from -4 to 4
- value_momentum: float32 [16, 4096, 1024], P('rep', 'fsdp', 'tp'), may hold values from -4 to 4
- key_cotangent: bfloat16 [16, 2048, 1024], P('rep', 'fsdp', 'tp'), may hold values from -6 to 6
- value_cotangent: bfloat16 [16, 2048, 1024], P('rep', 'fsdp', 'tp'), may hold values from -6 to 6
- step_number: int32 [1], replicated, may hold values from 0 to 999
Outputs:
- projected_keys: bfloat16 [16, 2048, 1024], P('rep', 'fsdp', 'tp')
- projected_values: bfloat16 [16, 2048, 1024], P('rep', 'fsdp', 'tp')
- averaged_key_weight: float32 [16, 4096, 1024], P('rep', 'fsdp', 'tp')
- averaged_value_weight: float32 [16, 4096, 1024], P('rep', 'fsdp', 'tp')
- key_velocity: float32 [16, 4096, 1024], P('rep', 'fsdp', 'tp')
- value_velocity: float32 [16, 4096, 1024], P('rep', 'fsdp', 'tp')
The draws below stay inside these ranges and needn't reach their ends.
All inputs are finite; a program needn't handle non-finite values.
Results may differ from the reference program's by a relative error of at most 0.005.
Values may be sent and summed in bfloat16 or wider, within the bound.
No kernel may reach another device: no remote copies, remote signals or barrier semaphores. Data moves between devices by JAX's collectives and lax.ppermute only.
A program may use at most 64 MiB of HBM per device.

```python
import jax
import jax.numpy as jnp
from jax import lax

D = 4096
KV = 1024
TOKENS = 2048
REPS = 16


def block_scale(key, dims, cuts, low, high):
    def one(axis_at, shards_of):
        steps = jax.random.uniform(jax.random.fold_in(jax.random.fold_in(key, 6), axis_at), (shards_of,), jnp.float32, low / len(cuts), high / len(cuts))
        return jnp.repeat(jnp.exp(steps), dims[axis_at] // shards_of).reshape((-1,) + (1,) * (len(dims) - axis_at - 1))

    level = one(*cuts[0])
    for cut in cuts[1:]:
        level = level * one(*cut)
    return level


def bell_draw(rng, dims, spread, most, pieces=(), held_as=jnp.bfloat16):
    values = jax.random.normal(rng, dims, jnp.float32) * spread
    if len(pieces) > 0:
        values = block_scale(rng, dims, pieces, -0.22, 0.18) * values
    return jnp.clip(values, min=-most, max=most).astype(held_as)


def setup_inputs(seed: int = 0) -> dict:
    keys = jax.random.split(jax.random.key(seed), 9)
    tokens = bell_draw(keys[0], (REPS, TOKENS, D), 1.0, 6.0, ((0, 16), (1, 8), (2, 4)))
    key_weight = bell_draw(keys[1], (REPS, D, KV), 1.0, 6.0, ((0, 16), (1, 8), (2, 4)), jnp.float32)
    value_weight = bell_draw(keys[2], (REPS, D, KV), 1.0, 6.0, ((0, 16), (1, 8), (2, 4)), jnp.float32)
    key_momentum = bell_draw(keys[3], (REPS, D, KV), 0.5, 4.0, ((0, 16), (1, 8), (2, 4)), jnp.float32)
    value_momentum = bell_draw(keys[4], (REPS, D, KV), 0.5, 4.0, ((0, 16), (1, 8), (2, 4)), jnp.float32)
    key_cotangent = bell_draw(keys[5], (REPS, TOKENS, KV), 1.0, 6.0, ((0, 16), (1, 8), (2, 4)))
    value_cotangent = bell_draw(keys[6], (REPS, TOKENS, KV), 1.0, 6.0, ((0, 16), (1, 8), (2, 4)))
    step_number = jax.random.randint(keys[7], (1,), 0, 1000).astype(jnp.int32)
    return dict(tokens=tokens, key_weight=key_weight, value_weight=value_weight, key_momentum=key_momentum, value_momentum=value_momentum, key_cotangent=key_cotangent, value_cotangent=value_cotangent, step_number=step_number)


momentum_decay = 0.9


def one_replica(items):
    inputs, key_w, value_w, key_m, value_m, key_c, value_c = items
    scale = D ** -0.5
    keys_out = (jnp.dot(inputs, key_w.astype(jnp.bfloat16), preferred_element_type=jnp.float32) * scale).astype(jnp.bfloat16)
    values_out = (jnp.dot(inputs, value_w.astype(jnp.bfloat16), preferred_element_type=jnp.float32) * scale).astype(jnp.bfloat16)
    key_grad = jnp.dot(inputs.T, key_c, preferred_element_type=jnp.float32) * scale
    value_grad = jnp.dot(inputs.T, value_c, preferred_element_type=jnp.float32) * scale
    key_vel = momentum_decay * key_m + key_grad
    value_vel = momentum_decay * value_m + value_grad
    return keys_out, values_out, key_vel, value_vel


def reference(tokens, key_weight, value_weight, key_momentum, value_momentum, key_cotangent, value_cotangent, step_number):
    keys_out, values_out, key_vel, value_vel = lax.map(
        one_replica, (tokens, key_weight, value_weight, key_momentum, value_momentum, key_cotangent, value_cotangent))
    learn = 0.5 * (step_number[0].astype(jnp.float32) + 1.0) / 1000.0
    key_moved = key_weight - learn * key_vel
    value_moved = value_weight - learn * value_vel
    distance = jnp.left_shift(jnp.int32(1), (step_number[0] % 4).astype(jnp.int32)) % REPS
    key_avg = 0.5 * (key_moved + jnp.roll(key_moved, distance, axis=0))
    value_avg = 0.5 * (value_moved + jnp.roll(value_moved, distance, axis=0))
    return keys_out, values_out, key_avg, value_avg, key_vel, value_vel
```

```python
from functools import partial

import jax
import jax.numpy as jnp
from jax import lax
from jax.experimental import pallas as pl
from jax.experimental.pallas import tpu as pltpu
from jax.sharding import PartitionSpec as P

D = 4096
scale = D ** (-0.5)
momentum_decay = 0.9
chunks = 2
bf16 = jnp.bfloat16
f32 = jnp.float32

vmem = pl.BlockSpec(memory_space=pltpu.VMEM)
smem = pl.BlockSpec(memory_space=pltpu.SMEM)


def call(kernel, outs, *operands, scratch=(), scalars=0, aliases=None, flops=0):
    moved = sum(a.size * a.dtype.itemsize for a in operands)
    moved += sum(o.size * o.dtype.itemsize for o in outs)
    return pl.pallas_call(
        kernel,
        out_shape=outs,
        in_specs=[smem] * scalars + [vmem] * (len(operands) - scalars),
        out_specs=[vmem] * len(outs),
        scratch_shapes=list(scratch),
        input_output_aliases=aliases or {},
        compiler_params=pltpu.CompilerParams(vmem_limit_bytes=24 * 2**20),
        cost_estimate=pl.CostEstimate(flops=flops, bytes_accessed=moved, transcendentals=0),
    )(*operands)


def like(shape, dtype):
    return jax.ShapeDtypeStruct(shape, dtype)


def across(block):
    return lax.ppermute(block, "fsdp", [(i, i ^ 1) for i in range(lax.axis_size("fsdp"))])


def around(block, hops):
    count = lax.axis_size("fsdp")
    return lax.ppermute(block, "fsdp", [(i, (i + 2 * hops) % count) for i in range(count)])


def swapped(block, mask):
    return lax.ppermute(block, "tp", [(i, i ^ mask) for i in range(lax.axis_size("tp"))])


def from_partner(block, distance):
    count = lax.axis_size("rep")
    return lax.ppermute(block, "rep", [(i, (i + distance) % count) for i in range(count)])


def split_kernel(core_ref, tokens_ref, own_ref, other_ref):
    half = own_ref.shape[1]
    core = core_ref[0]
    own_ref[...] = tokens_ref[0, :, pl.ds(pl.multiple_of(core * half, half), half)]
    other_ref[...] = tokens_ref[0, :, pl.ds(pl.multiple_of((1 - core) * half, half), half)]


def join_kernel(own_ref, other_ref, *part_refs):
    rows = own_ref.shape[0]
    for at, part in enumerate(part_refs):
        width = part.shape[1]
        part[:rows] = own_ref[:, at * width : (at + 1) * width]
        part[rows:] = other_ref[:, at * width : (at + 1) * width]


def beside_kernel(key_ref, value_ref, out_ref):
    width = key_ref.shape[2]
    out_ref[:, :width] = key_ref[0].astype(bf16)
    out_ref[:, width:] = value_ref[0].astype(bf16)


def partial_kernel(at_ref, a0, a1, a2, a3, cot_own, cot_other, p0, p1, p2, p3, held):
    tokens = cot_own.shape[0]
    for j, a in enumerate((a0, a1, a2, a3)):
        held[j] = a[...]
    for k, p in enumerate((p0, p1, p2, p3)):
        j = at_ref[k]
        total = lax.dot_general(
            held[j, :tokens], cot_own[...], (((0,), (0,)), ((), ())), preferred_element_type=f32
        )
        total += lax.dot_general(
            held[j, tokens:], cot_other[...], (((0,), (0,)), ((), ())), preferred_element_type=f32
        )
        p[...] = (total * scale).astype(p.dtype)


def update_kernel(
    at, learn_ref, p0, r1, r2, r3, kw, vw, km, vm, velocity_ref, moved_ref, short_ref
):
    rows = p0.shape[0]
    width = kw.shape[2]
    part = pl.ds(at * rows, rows)
    learn = learn_ref[0]
    gradient = p0[...] + r1[...].astype(f32) + r2[...].astype(f32) + r3[...].astype(f32)
    for i, (w, m) in enumerate(((kw, km), (vw, vm))):
        cols = slice(i * width, (i + 1) * width)
        velocity = momentum_decay * m[0, part] + gradient[:, cols]
        moved = w[0, part] - learn * velocity
        velocity_ref[:, cols] = velocity
        moved_ref[:, cols] = moved
        short_ref[:, cols] = moved.astype(bf16)


def finish_kernel(*refs):
    outs = refs[-4:]
    width = outs[0].shape[2]
    for at in range(chunks):
        velocity, moved, other = refs[3 * at : 3 * at + 3]
        rows = velocity.shape[0]
        part = pl.ds(at * rows, rows)
        averaged = 0.5 * (moved[...] + other[...].astype(f32))
        outs[0][0, part] = averaged[:, :width]
        outs[1][0, part] = averaged[:, width:]
        outs[2][0, part] = velocity[:, :width]
        outs[3][0, part] = velocity[:, width:]


def project_kernel(at_ref, *refs):
    acts, weights = refs[: 4 * chunks], refs[4 * chunks : 4 * chunks + 4]
    mine_ref, other_ref, held = refs[4 * chunks + 4 :]
    for i, a in enumerate(acts):
        held[i] = a[...]
    depth = held.shape[2]
    total = None
    for k, w in enumerate(weights):
        for at in range(chunks):
            term = jnp.dot(
                held[4 * at + at_ref[k]],
                w[at * depth : (at + 1) * depth],
                preferred_element_type=f32,
            )
            total = term if total is None else total + term
    rows = mine_ref.shape[0]
    mine_ref[...] = total[:rows]
    other_ref[...] = total[rows:].astype(bf16)


def project_end_kernel(mine_ref, other_ref, key_ref, value_ref):
    width = key_ref.shape[2]
    total = (mine_ref[...] + other_ref[...].astype(f32)) * scale
    key_ref[0] = total[:, :width].astype(bf16)
    value_ref[0] = total[:, width:].astype(bf16)


def step(tokens, kw, vw, km, vm, kc, vc, learn, core, order, distance):
    _, rows, features = tokens.shape
    _, depth, width = kw.shape
    half = features // 2
    both = 2 * width
    own, other = call(
        split_kernel, [like((rows, half), bf16)] * 2, core, tokens, scalars=1
    )
    arrived = across(other)
    cot_own = call(beside_kernel, [like((rows, both), bf16)], kc, vc)[0]
    weight = call(beside_kernel, [like((depth, both), bf16)], kw, vw)[0]
    parts = call(
        join_kernel, [like((2 * rows, half // chunks), bf16)] * chunks, own, arrived
    )
    cot_other = across(cot_own)
    weights = (weight, around(weight, -1), around(weight, 2), around(weight, 1))
    piece = depth // chunks
    kept, acts = [], []
    for at, a0 in enumerate(parts):
        a3 = swapped(a0, 3)
        a1 = swapped(a0, 1)
        a2 = swapped(a3, 1)
        acts += [a0, a1, a2, a3]
        p0, p1, p2, p3 = call(
            partial_kernel,
            [like((piece, both), f32)] + [like((piece, both), bf16)] * 3,
            order, a0, a1, a2, a3, cot_own, cot_other,
            scalars=1,
            scratch=[pltpu.VMEM((4,) + a0.shape, bf16)],
            flops=2 * 4 * piece * both * 2 * rows,
        )
        r1, r2, r3 = around(p1, 1), around(p2, 2), around(p3, -1)
        velocity, moved, short = call(
            partial(update_kernel, at),
            [like((piece, both), f32)] * 2 + [like((piece, both), bf16)],
            learn, p0, r1, r2, r3, kw, vw, km, vm,
            scalars=1,
        )
        kept += [velocity, moved, from_partner(short, distance)]
    mine, sent = call(
        project_kernel,
        [like((rows, both), f32), like((rows, both), bf16)],
        order, *acts, *weights,
        scalars=1,
        scratch=[pltpu.VMEM((4 * chunks,) + acts[0].shape, bf16)],
        flops=2 * 2 * rows * both * 4 * depth,
    )
    keys_out, values_out = call(
        project_end_kernel, [like((1, rows, width), bf16)] * 2, mine, across(sent)
    )
    averaged_key, averaged_value, key_velocity, value_velocity = call(
        finish_kernel, [like((1, depth, width), f32)] * 4, *kept
    )
    return keys_out, values_out, averaged_key, averaged_value, key_velocity, value_velocity


def body(tokens, kw, vw, km, vm, kc, vc, step_number):
    replicas = lax.axis_size("rep")
    at_x, core = lax.axis_index("fsdp") // 2, lax.axis_index("fsdp") % 2
    at_z = lax.axis_index("tp")
    order = jnp.stack([jnp.bitwise_xor((at_x + k) % 4, at_z) for k in range(4)]).astype(jnp.int32)
    learn = 0.5 * (step_number.astype(f32) + 1.0) / 1000.0
    branches = [partial(step, distance=2**power % replicas) for power in range(4)]
    return lax.switch(
        step_number[0] % 4,
        branches,
        tokens, kw, vw, km, vm, kc, vc, learn, core.reshape(1).astype(jnp.int32), order,
    )


def solution(mesh):
    spread = P("rep", "fsdp", "tp")
    return jax.shard_map(
        body,
        mesh=mesh,
        in_specs=(spread,) * 7 + (P(),),
        out_specs=(spread,) * 6,
        check_vma=False,
    )
```

```python
from functools import partial

import jax
import jax.numpy as jnp
from jax import lax
from jax.experimental import pallas as pl
from jax.experimental.pallas import tpu as pltpu
from jax.sharding import PartitionSpec as P

D = 4096
scale = D ** (-0.5)
momentum_decay = 0.9
chunks = 2
bf16 = jnp.bfloat16
f32 = jnp.float32

vmem = pl.BlockSpec(memory_space=pltpu.VMEM)
smem = pl.BlockSpec(memory_space=pltpu.SMEM)
anywhere = pl.BlockSpec(memory_space=pl.ANY)


def call(kernel, outs, *operands, scratch=(), scalars=0, late=(), flops=0):
    moved = sum(a.size * a.dtype.itemsize for a in operands)
    moved += sum(o.size * o.dtype.itemsize for o in outs)
    return pl.pallas_call(
        kernel,
        out_shape=outs,
        in_specs=[
            smem if i < scalars else anywhere if i in late else vmem for i in range(len(operands))
        ],
        out_specs=[vmem] * len(outs),
        scratch_shapes=list(scratch),
        compiler_params=pltpu.CompilerParams(vmem_limit_bytes=24 * 2**20),
        cost_estimate=pl.CostEstimate(flops=flops, bytes_accessed=moved, transcendentals=0),
    )(*operands)


def like(shape, dtype):
    return jax.ShapeDtypeStruct(shape, dtype)


def after(blocks, *others):
    count = len(blocks)
    late = range(count, count + len(others))
    outs = [like(block.shape, block.dtype) for block in blocks]
    return call(partial(pass_kernel, count), outs, *blocks, *others, late=late)


def across(block):
    return lax.ppermute(block, "fsdp", [(i, i ^ 1) for i in range(lax.axis_size("fsdp"))])


def around(block, mask):
    return lax.ppermute(block, "fsdp", [(i, i ^ (2 * mask)) for i in range(lax.axis_size("fsdp"))])


def swapped(block, mask):
    return lax.ppermute(block, "tp", [(i, i ^ mask) for i in range(lax.axis_size("tp"))])


def from_partner(block, distance):
    count = lax.axis_size("rep")
    return lax.ppermute(block, "rep", [(i, (i + distance) % count) for i in range(count)])


def split_kernel(core_ref, tokens_ref, key_ref, value_ref, own_ref, send_ref):
    half = own_ref.shape[1]
    width = key_ref.shape[2]
    core = core_ref[0]
    own_ref[...] = tokens_ref[0, :, pl.ds(pl.multiple_of(core * half, half), half)]
    send_ref[:, :half] = tokens_ref[0, :, pl.ds(pl.multiple_of((1 - core) * half, half), half)]
    send_ref[:, half : half + width] = key_ref[0]
    send_ref[:, half + width :] = value_ref[0]


def join_kernel(own_ref, arrived_ref, *part_refs):
    rows = own_ref.shape[0]
    for at, part in enumerate(part_refs):
        width = part.shape[1]
        part[:rows] = own_ref[:, at * width : (at + 1) * width]
        part[rows:] = arrived_ref[:, at * width : (at + 1) * width]


def beside_kernel(key_ref, value_ref, late_ref, out_ref):
    width = key_ref.shape[2]
    out_ref[:, :width] = key_ref[0].astype(bf16)
    out_ref[:, width:] = value_ref[0].astype(bf16)


def pass_kernel(count, *refs):
    for given, out in zip(refs[:count], refs[-count:]):
        out[...] = given[...]


def partial_kernel(at_ref, a0, a1, a2, a3, send, arrived, *refs):
    p0, p1, p2, p3, held = refs[-5:]
    tokens, features = send.shape
    cots = slice(features // 2, features)
    for j, a in enumerate((a0, a1, a2, a3)):
        held[j] = a[...]
    for k, p in enumerate((p0, p1, p2, p3)):
        j = at_ref[k]
        total = lax.dot_general(
            held[j, :tokens], send[:, cots], (((0,), (0,)), ((), ())), preferred_element_type=f32
        )
        total += lax.dot_general(
            held[j, tokens:], arrived[:, cots], (((0,), (0,)), ((), ())), preferred_element_type=f32
        )
        p[...] = (total * scale).astype(p.dtype)


def update_kernel(at, learn_ref, p0, r1, r3, r2, kw, vw, km, vm, *refs):
    velocity_ref, moved_ref, short_ref = refs[-3:]
    rows = p0.shape[0]
    width = kw.shape[2]
    part = pl.ds(at * rows, rows)
    learn = learn_ref[0]
    gradient = p0[...] + r1[...].astype(f32) + r2[...].astype(f32) + r3[...].astype(f32)
    for i, (w, m) in enumerate(((kw, km), (vw, vm))):
        cols = slice(i * width, (i + 1) * width)
        velocity = momentum_decay * m[0, part] + gradient[:, cols]
        moved = w[0, part] - learn * velocity
        velocity_ref[:, cols] = velocity
        moved_ref[:, cols] = moved
        short_ref[:, cols] = moved.astype(bf16)


def finish_kernel(*refs):
    outs = refs[-4:]
    width = outs[0].shape[2]
    for at in range(chunks):
        velocity, moved, other = refs[3 * at : 3 * at + 3]
        rows = velocity.shape[0]
        part = pl.ds(at * rows, rows)
        averaged = 0.5 * (moved[...] + other[...].astype(f32))
        outs[0][0, part] = averaged[:, :width]
        outs[1][0, part] = averaged[:, width:]
        outs[2][0, part] = velocity[:, :width]
        outs[3][0, part] = velocity[:, width:]


def project_kernel(at_ref, late_ref, *refs):
    acts, weights = refs[: 4 * chunks], refs[4 * chunks : 4 * chunks + 4]
    mine_ref, other_ref, held = refs[4 * chunks + 4 :]
    for i, a in enumerate(acts):
        held[i] = a[...]
    depth = held.shape[2]
    total = None
    for m, w in enumerate(weights):
        for at in range(chunks):
            term = jnp.dot(
                held[4 * at + at_ref[m]],
                w[at * depth : (at + 1) * depth],
                preferred_element_type=f32,
            )
            total = term if total is None else total + term
    rows = mine_ref.shape[0]
    mine_ref[...] = total[:rows]
    other_ref[...] = total[rows:].astype(bf16)


def project_end_kernel(mine_ref, other_ref, key_ref, value_ref):
    width = key_ref.shape[2]
    total = (mine_ref[...] + other_ref[...].astype(f32)) * scale
    key_ref[0] = total[:, :width].astype(bf16)
    value_ref[0] = total[:, width:].astype(bf16)


def step(tokens, kw, vw, km, vm, kc, vc, learn, core, order, distance):
    _, rows, features = tokens.shape
    _, depth, width = kw.shape
    half = features // 2
    both = 2 * width
    own, send = call(
        split_kernel,
        [like((rows, half), bf16), like((rows, half + both), bf16)],
        core, tokens, kc, vc,
        scalars=1,
    )
    arrived = across(send)
    weight = call(beside_kernel, [like((depth, both), bf16)], kw, vw, arrived, late=[2])[0]
    a0, b0 = call(
        join_kernel, [like((2 * rows, half // chunks), bf16)] * chunks, own, arrived
    )
    piece = depth // chunks

    def partials(a0, a1, a2, a3, *others):
        return call(
            partial_kernel,
            [like((piece, both), f32)] + [like((piece, both), bf16)] * 3,
            order, a0, a1, a2, a3, send, arrived, *others,
            scalars=1,
            late=range(7, 7 + len(others)),
            scratch=[pltpu.VMEM((4,) + a0.shape, bf16)],
            flops=2 * 4 * piece * both * 2 * rows,
        )

    def reduced(p1, p2, p3):
        parts = p1, p2, p3
        return [around(parts[m - 1], m) for m in (2, 1, 3)]

    def updated(at, late, parts):
        return call(
            partial(update_kernel, at),
            [like((piece, both), f32)] * 2 + [like((piece, both), bf16)],
            learn, *parts, kw, vw, km, vm, *late,
            scalars=1,
            late=range(9, 9 + len(late)),
        )

    a3, a1 = swapped(a0, 3), swapped(a0, 1)
    a2 = swapped(a3, 1)
    b3, b1 = swapped(b0, 3), swapped(after([b0], a3)[0], 1)
    swaps = [around(weight, m) for m in (3, 1, 2)]
    weights = weight, swaps[1], swaps[2], swaps[0]
    own_a, *parts_a = partials(a0, a1, a2, a3)
    b2 = swapped(after([b3], own_a, *swaps)[0], 1)
    velocity_a, moved_a, short_a = updated(0, (), (own_a, *reduced(*parts_a)))
    partner_a = from_partner(short_a, distance)
    own_b, *parts_b = partials(b0, b1, b2, b3)
    parts_b = after(parts_b, short_a)
    own_b = after([own_b], partner_a)[0]
    velocity_b, moved_b, short_b = updated(1, (), (own_b, *reduced(*parts_b)))
    partner_b = from_partner(short_b, distance)
    partner_b = after([partner_b])[0]
    kept = [velocity_a, moved_a, partner_a, velocity_b, moved_b, partner_b]
    mine, sent = call(
        project_kernel,
        [like((rows, both), f32), like((rows, both), bf16)],
        order, short_b, a0, a1, a2, a3, b0, b1, b2, b3, *weights,
        scalars=1,
        late=[1],
        scratch=[pltpu.VMEM((4 * chunks,) + a0.shape, bf16)],
    )
    keys_out, values_out = call(
        project_end_kernel, [like((1, rows, width), bf16)] * 2, mine, across(sent)
    )
    averaged_key, averaged_value, key_velocity, value_velocity = call(
        finish_kernel, [like((1, depth, width), f32)] * 4, *kept
    )
    return keys_out, values_out, averaged_key, averaged_value, key_velocity, value_velocity


def body(tokens, kw, vw, km, vm, kc, vc, step_number):
    replicas = lax.axis_size("rep")
    at_x, core = lax.axis_index("fsdp") // 2, lax.axis_index("fsdp") % 2
    at_z = lax.axis_index("tp")
    order = jnp.stack([at_x ^ at_z ^ m for m in range(4)]).astype(jnp.int32)
    learn = 0.5 * (step_number.astype(f32) + 1.0) / 1000.0
    branches = [partial(step, distance=2**power % replicas) for power in range(4)]
    return lax.switch(
        step_number[0] % 4,
        branches,
        tokens, kw, vw, km, vm, kc, vc, learn, core.reshape(1).astype(jnp.int32), order,
    )


def solution(mesh):
    spread = P("rep", "fsdp", "tp")
    return jax.shard_map(
        body,
        mesh=mesh,
        in_specs=(spread,) * 7 + (P(),),
        out_specs=(spread,) * 6,
        check_vma=False,
    )
```
